256 devices in a mesh: blk: 2 (over x_lo), pb: 128 (over z, y, x_hi, core).
Axes of the slice: x: 4 (x_hi: 2, x_lo: 2; x = x_hi * 2 + x_lo), y: 4, z: 8, core: 2. Of those that a mesh axis runs over, the one named last changes fastest.
Arguments:
- hidden: bfloat16 [128, 128, 4096], P('pb', 'blk'), may hold values from -24 to 24
- query: bfloat16 [128, 128, 2048], P('pb', 'blk'), may hold values from -37 to 37
- out_grad: bfloat16 [128, 128, 2048], P('pb', 'blk'), may hold values from -6 to 6
- attn_out: bfloat16 [128, 128, 2048], P('pb', 'blk'), may hold values from -6 to 6
- keys: bfloat16 [128, 4, 256, 2048], P('pb', 'blk'), may hold values from -4 to 4
- values: bfloat16 [128, 4, 256, 2048], P('pb', 'blk'), may hold values from -6 to 6
- lengths: int32 [128, 4], P('pb', 'blk'), may hold values from 1 to 256, as said below
- w_query: bfloat16 [4096, 2048], P('pb', 'blk'), may hold values from -0.09375 to 0.09375
Outputs:
- hidden_grad: bfloat16 [128, 128, 4096], P('pb', 'blk')
- key_grad: bfloat16 [128, 4, 256, 2048], P('pb', 'blk')
- value_grad: bfloat16 [128, 4, 256, 2048], P('pb', 'blk')
- w_query_grad: float32 [4096, 2048], P('pb', 'blk')
The draws below stay inside these ranges and needn't reach their ends.
Inputs may be any that keep to these rules, and one draw needn't show every extreme that they name: `lengths`: every passage has at least one valid token, and every question has a passage with all 256 tokens valid.
All inputs are finite; a program needn't handle non-finite values.
Results may differ from the reference program's by a relative error of at most 0.0056.
Values may be sent and summed in bfloat16 or wider, within the bound.
No kernel may reach another device: no remote copies, remote signals or barrier semaphores. Data moves between devices by JAX's collectives and lax.ppermute only.
A program may use at most 128 MiB of HBM per device.

```python
import jax
import jax.numpy as jnp
from jax import lax

D = 4096
HDIM = 64
HEADS = 32
PLEN = 256
HD = 2048
DEC = 128
PASSAGES = 4
QUESTIONS = 128


def draw_query(key, part):
    key = jax.random.fold_in(key, 11)
    base = jax.random.truncated_normal(key, -4.0, 4.0, (QUESTIONS, DEC, HD), jnp.float32)
    return base.astype(jnp.bfloat16)


def draw_keys(key, part):
    key = jax.random.fold_in(key, 12)
    base = jax.random.truncated_normal(key, -4.0, 4.0, (QUESTIONS, PASSAGES, PLEN, HD), jnp.float32)
    return base.astype(jnp.bfloat16)


def draw_lengths(key, part):
    key = jax.random.fold_in(key, 13)
    first_key, second_key = jax.random.split(key)
    counts = jax.random.randint(first_key, (QUESTIONS, PASSAGES), 1, PLEN + 1, dtype=jnp.int32)
    full_one = jax.random.randint(second_key, (QUESTIONS, 1), 0, PASSAGES, dtype=jnp.int32)
    passage = jnp.arange(PASSAGES, dtype=jnp.int32)[None, :]
    return jnp.where(passage == full_one, PLEN, counts).astype(jnp.int32)


def with_spikes(drawn, key, source, target, blocks, factor):
    owner, partner = [(jnp.arange(drawn.shape[axis_at]) // (drawn.shape[axis_at] // blocks)).reshape([-1 if axis == axis_at else 1 for axis in range(drawn.ndim)]) for axis_at in (source, target)]
    chosen = jax.random.permutation(key, blocks)[partner]
    strong = (owner == chosen) | (owner == (partner + blocks // 2) % blocks)
    return jnp.where(strong, factor * drawn, drawn)


def shard_levels(stream_key, extent, cuts, smallest, top_value):
    factor_of, own = 1.0, jax.random.fold_in(stream_key, 6)
    for position, parts in cuts:
        steps = jnp.exp(jax.random.uniform(jax.random.fold_in(own, position), (parts,), jnp.float32, smallest / len(cuts), top_value / len(cuts)))
        factor_of = factor_of * jnp.repeat(steps, extent[position] // parts).reshape([-1 if axis == position else 1 for axis in range(len(extent))])
    return factor_of


def scatter_about(own_key, extent, width, reach, cuts=(), kind=jnp.bfloat16):
    drawn = jax.random.normal(own_key, extent, jnp.float32) * width
    if len(cuts) > 0:
        drawn = shard_levels(own_key, extent, cuts, -0.22, 0.18) * drawn
    return jnp.clip(drawn, min=-reach, max=reach).astype(kind)


def noise_with(key, dims, deviation, most, shards, heavy, held_as=jnp.bfloat16):
    array = deviation * jax.random.normal(key, dims, jnp.float32)
    if shards:
        array = array * shard_levels(key, dims, shards, -0.22, 0.18)
    return jnp.clip(with_spikes(array, jax.random.fold_in(key, 3), *heavy), -most, most).astype(held_as)


def setup_inputs(seed: int = 0) -> dict:
    key_list = jax.random.split(jax.random.key(seed), 9)
    hidden = noise_with(key_list[0], (QUESTIONS, DEC, D), 1.0, 24.0, ((0, 128), (1, 2)), (0, 2, 128, 5.5))
    query = draw_query(jax.random.fold_in(key_list[8], 71), 0)
    out_grad = scatter_about(key_list[2], (QUESTIONS, DEC, HD), 1.0, 6.0, ((0, 128), (1, 2)))
    attn_out = scatter_about(key_list[3], (QUESTIONS, DEC, HD), 1.0, 6.0, ((0, 128), (1, 2)))
    keys = draw_keys(jax.random.fold_in(key_list[8], 71), 0)
    values = scatter_about(key_list[5], (QUESTIONS, PASSAGES, PLEN, HD), 1.0, 6.0, ((0, 128), (1, 2)))
    lengths = draw_lengths(jax.random.fold_in(key_list[8], 71), 0)
    w_query = scatter_about(key_list[7], (D, HD), D ** -0.5, 0.09375, ((0, 128), (1, 2)))
    return dict(hidden=hidden, query=query, out_grad=out_grad, attn_out=attn_out, keys=keys, values=values, lengths=lengths, w_query=w_query)


SCORE_SCALE = 0.125
NEGATIVE = -1e30


def key_valid_of(passage_lengths, passage_len):
    tokens = jnp.arange(passage_len, dtype=jnp.int32)
    return (tokens[None, :] < passage_lengths[:, None]).reshape(-1)


def one_question(items):
    query_q, grad_q, output_q, keys_q, values_q, lengths_q = items
    key_valid = key_valid_of(lengths_q, PLEN)
    query_rows = query_q.astype(jnp.float32).reshape(DEC, HEADS, HDIM)
    grad_rows = grad_q.astype(jnp.float32).reshape(DEC, HEADS, HDIM)
    output_rows = output_q.astype(jnp.float32).reshape(DEC, HEADS, HDIM)
    key_rows = keys_q.astype(jnp.float32).reshape(PASSAGES * PLEN, HEADS, HDIM)
    value_rows = values_q.astype(jnp.float32).reshape(PASSAGES * PLEN, HEADS, HDIM)
    scores = jnp.einsum('qhd,khd->hqk', query_rows, key_rows) * SCORE_SCALE
    scores = jnp.where(key_valid[None, None, :], scores, NEGATIVE)
    row_max = jnp.max(scores, axis=-1)
    row_total = jnp.sum(jnp.exp(scores - row_max[:, :, None]), axis=-1)
    log_total = row_max + jnp.log(row_total)
    probs = jnp.where(key_valid[None, None, :], jnp.exp(scores - log_total[:, :, None]), 0.0)
    probs_low = lax.optimization_barrier(probs.astype(jnp.bfloat16)).astype(jnp.float32)
    value_grad = jnp.einsum('hqk,qhd->khd', probs_low, grad_rows).astype(jnp.bfloat16)
    prob_grad = jnp.einsum('qhd,khd->hqk', grad_rows, value_rows)
    row_delta = jnp.transpose(jnp.sum(grad_rows * output_rows, axis=2))
    score_grad = (probs * (prob_grad - row_delta[:, :, None]) * SCORE_SCALE).astype(jnp.bfloat16)
    score_grad = lax.optimization_barrier(score_grad).astype(jnp.float32)
    key_grad = jnp.einsum('hqk,qhd->khd', score_grad, query_rows).astype(jnp.bfloat16)
    query_grad = jnp.einsum('hqk,khd->qhd', score_grad, key_rows).astype(jnp.bfloat16)
    return (query_grad.reshape(DEC, HD), key_grad.reshape(PASSAGES, PLEN, HD),
            value_grad.reshape(PASSAGES, PLEN, HD))


def reference(hidden, query, out_grad, attn_out, keys, values, lengths, w_query):
    query_grad, key_grad, value_grad = lax.map(
        one_question, (query, out_grad, attn_out, keys, values, lengths))
    flat_grad = query_grad.reshape(QUESTIONS * DEC, HD)
    flat_hidden = hidden.reshape(QUESTIONS * DEC, D)
    hidden_grad = jnp.dot(flat_grad, w_query.T, preferred_element_type=jnp.float32)
    hidden_grad = hidden_grad.astype(jnp.bfloat16).reshape(QUESTIONS, DEC, D)
    w_query_grad = jnp.dot(flat_hidden.T, flat_grad, preferred_element_type=jnp.float32)
    return hidden_grad, key_grad, value_grad, w_query_grad
```

```python
import functools

import jax
import jax.numpy as jnp
import numpy as np
from jax import lax
from jax.experimental import pallas as pl
from jax.experimental.pallas import tpu as pltpu
from jax.sharding import PartitionSpec as P

HDIM = 64
PAIR = 2 * HDIM
SCORE_SCALE = 0.125
LOG2E = float(np.log2(np.e))
SCORE_LOG2 = SCORE_SCALE * LOG2E
NEGATIVE = -1e30
FACTORS = (8, 4, 2, 2)
VMEM_LIMIT = 32 * 1024 * 1024
STAT_ROWS = 8

NT = (((1,), (1,)), ((), ()))
NN = (((1,), (0,)), ((), ()))


def dot(lhs, rhs, dims):
    return lax.dot_general(lhs, rhs, dims, preferred_element_type=jnp.float32)


def head_masks():
    lane = lax.broadcasted_iota(jnp.int32, (1, PAIR), 1)
    first = (lane < HDIM).astype(jnp.float32)
    return first.astype(jnp.bfloat16), (1.0 - first).astype(jnp.bfloat16)


def by_head(rows):
    first, second = head_masks()
    return [rows * first, rows * second]


def valid_keys(lengths, passage_len, shape):
    token = lax.broadcasted_iota(jnp.int32, shape, 0)
    limit = jnp.full(shape, lengths[0], jnp.int32)
    for passage in range(1, len(lengths)):
        limit = jnp.where(
            token >= passage * passage_len, passage * passage_len + lengths[passage], limit
        )
    return token < limit


def local_stats(stacked, key_pair, lengths, passage_len):
    scores = dot(key_pair, stacked, NT) * SCORE_LOG2
    scores = jnp.where(valid_keys(lengths, passage_len, scores.shape), scores, NEGATIVE)
    row_max = jnp.max(scores, axis=0, keepdims=True)
    row_total = jnp.sum(jnp.exp2(scores - row_max), axis=0, keepdims=True)
    return row_max, row_total


def own_stats_kernel(pairs, passage_len, passages, len_ref, q_ref, k_ref, g_ref, o_ref, out_ref):
    lengths = [len_ref[i] for i in range(passages)]
    for j in range(pairs):
        cols = slice(j * PAIR, (j + 1) * PAIR)
        stacked = jnp.concatenate(by_head(q_ref[:, cols]), axis=0)
        row_max, row_total = local_stats(stacked, k_ref[:, cols], lengths, passage_len)
        product = g_ref[:, cols].astype(jnp.float32) * o_ref[:, cols].astype(jnp.float32)
        lane = lax.broadcasted_iota(jnp.int32, product.shape, 1)
        both = jnp.concatenate(
            [jnp.where(lane < HDIM, product, 0.0), jnp.where(lane < HDIM, 0.0, product)], axis=0
        )
        delta = jnp.sum(jnp.transpose(both), axis=0, keepdims=True)
        out_ref[j, 0:1, :] = row_max
        out_ref[j, 1:2, :] = row_total
        out_ref[j, 2:3, :] = delta
        out_ref[j, 3:STAT_ROWS, :] = jnp.zeros((STAT_ROWS - 3, row_max.shape[1]), jnp.float32)


def peer_stats_kernel(pairs, passage_len, passages, len_ref, q_ref, k_ref, own_ref, out_ref):
    lengths = [len_ref[i] for i in range(passages)]
    for j in range(pairs):
        cols = slice(j * PAIR, (j + 1) * PAIR)
        stacked = jnp.concatenate(by_head(q_ref[:, cols]), axis=0)
        row_max, row_total = local_stats(stacked, k_ref[:, cols], lengths, passage_len)
        out_ref[j] = own_ref[j]
        out_ref[j, 3:4, :] = row_max
        out_ref[j, 4:5, :] = row_total


def stats_call(kernel, lengths, key_rows, row_arrays, stat_arrays, passage_len, pairs):
    tokens, hd = key_rows.shape
    rows = row_arrays[0].shape[0]
    total_pairs = hd // PAIR
    wide = pairs * PAIR
    row_spec = pl.BlockSpec((rows, wide), lambda i, s: (0, i))
    key_spec = pl.BlockSpec((tokens, wide), lambda i, s: (0, i))
    stat_spec = pl.BlockSpec((pairs, STAT_ROWS, 2 * rows), lambda i, s: (i, 0, 0))
    return pl.pallas_call(
        functools.partial(kernel, pairs, passage_len, lengths.shape[0]),
        out_shape=jax.ShapeDtypeStruct((total_pairs, STAT_ROWS, 2 * rows), jnp.float32),
        grid_spec=pltpu.PrefetchScalarGridSpec(
            num_scalar_prefetch=1,
            grid=(total_pairs // pairs,),
            in_specs=[row_spec, key_spec]
            + [row_spec] * (len(row_arrays) - 1)
            + [stat_spec] * len(stat_arrays),
            out_specs=stat_spec,
        ),
        compiler_params=pltpu.CompilerParams(vmem_limit_bytes=VMEM_LIMIT),
        cost_estimate=pl.CostEstimate(
            flops=16 * rows * tokens * hd, bytes_accessed=2 * tokens * hd, transcendentals=0
        ),
    )(lengths, row_arrays[0], key_rows, *row_arrays[1:], *stat_arrays)


def grad_kernel(
    pairs, passage_len, passages, carried, s_ref, mine_ref, theirs_ref, qo_ref, qp_ref, go_ref,
    gp_ref, k_ref, v_ref, *rest
):
    dq_ref, dk_ref, dv_ref = rest[2:] if carried else rest
    lengths = [s_ref[1 + i] for i in range(passages)]
    rows = qo_ref.shape[0]
    for j in range(pairs):
        cols = slice(j * PAIR, (j + 1) * PAIR)
        mine, theirs = mine_ref[j], theirs_ref[j]

        def log_total(first_max, first_total, second_max, second_total):
            top = jnp.maximum(first_max, second_max)
            total = first_total * jnp.exp2(first_max - top) + second_total * jnp.exp2(
                second_max - top
            )
            return top + jnp.log2(total)

        lse = jnp.concatenate(
            [
                log_total(mine[0:1], mine[1:2], theirs[3:4], theirs[4:5]),
                log_total(mine[3:4], mine[4:5], theirs[0:1], theirs[1:2]),
            ],
            axis=1,
        )
        delta = jnp.concatenate([mine[2:3], theirs[2:3]], axis=1)
        queries = jnp.concatenate(by_head(qo_ref[:, cols]) + by_head(qp_ref[:, cols]), axis=0)
        grads = jnp.concatenate(by_head(go_ref[:, cols]) + by_head(gp_ref[:, cols]), axis=0)
        key_pair = k_ref[:, cols]
        scores = dot(key_pair, queries, NT)
        probs = jnp.exp2(scores * SCORE_LOG2 - lse)
        probs = jnp.where(valid_keys(lengths, passage_len, scores.shape), probs, 0.0)
        dv_ref[:, cols] = dot(probs.astype(jnp.bfloat16), grads, NN).astype(jnp.bfloat16)
        prob_grad = dot(v_ref[:, cols], grads, NT)
        score_grad = (probs * (prob_grad - delta)).astype(jnp.bfloat16)
        dk_ref[:, cols] = (dot(score_grad, queries, NN) * SCORE_SCALE).astype(jnp.bfloat16)
        query_t = dot(jnp.transpose(key_pair), score_grad, NN) * SCORE_SCALE
        query_grad = jnp.transpose(query_t)
        lane = lax.broadcasted_iota(jnp.int32, (rows, PAIR), 1)
        for which in range(2):
            at = which * 2 * rows
            dq_ref[which, :, cols] = jnp.where(
                lane < HDIM, query_grad[at : at + rows], query_grad[at + rows : at + 2 * rows]
            ).astype(dq_ref.dtype)


def grad_call(scalars, mine, theirs, rows4, key_rows, value_rows, carried, dq_type, passage_len,
              passages, pairs):
    tokens, hd = key_rows.shape
    rows = rows4[0].shape[0]
    half = hd // 2
    wide = pairs * PAIR
    steps = half // wide
    row_spec = pl.BlockSpec((rows, wide), lambda i, s: (0, s[0] * steps + i))
    key_spec = pl.BlockSpec((tokens, wide), lambda i, s: (0, s[0] * steps + i))
    stat_spec = pl.BlockSpec(
        (pairs, STAT_ROWS, 2 * rows), lambda i, s: (s[0] * steps + i, 0, 0)
    )
    any_spec = pl.BlockSpec(memory_space=pl.ANY)
    grad_shape = jax.ShapeDtypeStruct((tokens, hd), jnp.bfloat16)
    return pl.pallas_call(
        functools.partial(grad_kernel, pairs, passage_len, passages, len(carried) > 0),
        out_shape=(jax.ShapeDtypeStruct((2, rows, half), dq_type), grad_shape, grad_shape),
        grid_spec=pltpu.PrefetchScalarGridSpec(
            num_scalar_prefetch=1,
            grid=(steps,),
            in_specs=[stat_spec] * 2 + [row_spec] * 4 + [key_spec] * 2
            + [any_spec] * len(carried),
            out_specs=(
                pl.BlockSpec((2, rows, wide), lambda i, s: (0, 0, i)), key_spec, key_spec
            ),
        ),
        input_output_aliases={9: 1, 10: 2} if carried else {},
        compiler_params=pltpu.CompilerParams(vmem_limit_bytes=VMEM_LIMIT),
        cost_estimate=pl.CostEstimate(
            flops=40 * rows * tokens * hd, bytes_accessed=4 * tokens * hd, transcendentals=0
        ),
    )(scalars, mine, theirs, *rows4, key_rows, value_rows, *carried)


def on_device(hidden, query, out_grad, attn_out, keys, values, lengths, w_query):
    nz, ny, nx, nc = FACTORS
    plane = ny * nx * nc
    blk, pb = lax.axis_index("blk"), lax.axis_index("pb")
    z_at, core = pb // plane, lax.rem(pb, nc)
    plane_groups = [[z * plane + r for r in range(plane)] for z in range(nz)]

    def other_blk(x):
        return lax.ppermute(x, "blk", [(0, 1), (1, 0)])

    def other_core(x):
        return lax.ppermute(x, "pb", [(i, i ^ 1) for i in range(nz * plane)])

    def from_z(x, offset):
        total = nz * plane
        return lax.ppermute(
            x, "pb", [(i, (i - offset * plane) % total) for i in range(total)]
        )

    tokens = keys.shape[1] * keys.shape[2]
    passages, passage_len = keys.shape[1], keys.shape[2]
    hd = keys.shape[3]
    rows, width = hidden.shape[1], hidden.shape[2]
    key_rows, value_rows = keys.reshape(tokens, hd), values.reshape(tokens, hd)
    q_own, g_own, o_own = query[0], out_grad[0], attn_out[0]

    q_peer = other_blk(q_own)
    g_peer = other_blk(g_own)

    w_tile = lax.all_gather(w_query, "pb", axis=0, tiled=True, axis_index_groups=plane_groups)
    tile = width // nz

    q_peer, hidden_rows = lax.optimization_barrier((q_peer, hidden[0]))

    def column_block(offset):
        at = lax.rem(z_at + (nz - offset), nz) * tile
        return lax.dynamic_slice_in_dim(hidden_rows, at, tile, axis=1)

    hidden_own = jnp.stack(
        [column_block(0)] + [from_z(column_block(s), s) for s in range(1, nz)], axis=0
    )
    hidden_peer = other_blk(hidden_own)
    hidden_t = jnp.transpose(
        jnp.concatenate([hidden_own, hidden_peer], axis=1).reshape(nz * 2 * rows, tile)
    )

    lens = lengths[0]
    stat_pairs = min(4, hd // PAIR)
    stats_own = stats_call(
        own_stats_kernel, lens, key_rows, [q_own, g_own, o_own], [], passage_len, stat_pairs
    )
    mine = stats_call(
        peer_stats_kernel, lens, key_rows, [q_peer], [stats_own], passage_len, stat_pairs
    )
    theirs = other_blk(mine)

    rows4 = [q_own, q_peer, g_own, g_peer]
    grad_pairs = min(2, hd // PAIR // 2)

    def half_grad(which, carried, dq_type):
        scalars = jnp.concatenate([jnp.reshape(which, (1,)), lens]).astype(jnp.int32)
        return grad_call(scalars, mine, theirs, rows4, key_rows, value_rows, carried, dq_type,
                         passage_len, passages, grad_pairs)

    dq_send, key_part, value_part = half_grad(1 - blk, (), jnp.bfloat16)
    dq_here, key_grad, value_grad = half_grad(blk, (key_part, value_part), jnp.float32)
    dq_there = other_blk(dq_send)
    qg_own = (dq_here[0] + dq_there[1].astype(jnp.float32)).astype(jnp.bfloat16)
    qg_peer = (dq_here[1] + dq_there[0].astype(jnp.float32)).astype(jnp.bfloat16)

    qg_own, qg_peer, hidden_t = lax.optimization_barrier((qg_own, qg_peer, hidden_t))

    blocks = [[None] * nz, [None] * nz]
    for part, start in enumerate((qg_own, qg_peer)):
        blocks[part][0] = start
    ups, downs = (nz // 2, nz - 1 - nz // 2), (nz - 1 - nz // 2, nz // 2)
    for step in range(1, nz // 2 + 1):
        for part in range(2):
            if step <= ups[part]:
                blocks[part][step] = from_z(blocks[part][step - 1], 1)
            if step <= downs[part]:
                blocks[part][nz - step] = from_z(blocks[part][(nz - step + 1) % nz], -1)
    qg_all = jnp.concatenate([blocks[part][s] for s in range(nz) for part in range(2)], axis=0)

    w_term = lax.dot_general(hidden_t, qg_all, NN, preferred_element_type=jnp.float32)
    state_term = lax.dot_general(qg_all, w_tile, NT, preferred_element_type=jnp.float32)

    w_term = w_term.reshape(ny * nx, nc, -1, w_term.shape[1])
    kept = lax.dynamic_index_in_dim(w_term, core, axis=1, keepdims=False)
    given = lax.dynamic_index_in_dim(w_term, 1 - core, axis=1, keepdims=False)
    w_sum = (kept + other_core(given)).astype(jnp.bfloat16)
    plane_at = lax.rem(pb, plane) // nc

    def across_plane(flip):
        block = lax.dynamic_index_in_dim(w_sum, plane_at ^ flip, axis=0, keepdims=False)
        if flip == 0:
            return block
        return lax.ppermute(block, "pb", [(i, i ^ (flip * nc)) for i in range(nz * plane)])

    w_query_grad = sum(across_plane(flip).astype(jnp.float32) for flip in range(ny * nx))

    state_term = state_term.reshape(nz, 2, rows, tile)
    state_sum = state_term[:, 0] + other_blk(state_term[:, 1].astype(jnp.bfloat16)).astype(
        jnp.float32
    )
    state_sum = state_sum.astype(jnp.bfloat16)
    arrived = [state_sum[0]] + [from_z(state_sum[nz - s], s) for s in range(1, nz)]
    state_all = lax.dynamic_slice_in_dim(
        jnp.stack(arrived + arrived, axis=0), lax.rem(nz - z_at, nz), nz, axis=0
    )
    hidden_grad = jnp.transpose(state_all, (1, 0, 2)).reshape(hidden.shape)
    return (hidden_grad, key_grad.reshape(keys.shape), value_grad.reshape(values.shape),
            w_query_grad)


def solution(mesh):
    return jax.shard_map(
        on_device,
        mesh=mesh,
        in_specs=(
            P("pb", "blk", None),
            P("pb", "blk", None),
            P("pb", "blk", None),
            P("pb", "blk", None),
            P("pb", "blk", None, None),
            P("pb", "blk", None, None),
            P("pb", "blk"),
            P("pb", "blk"),
        ),
        out_specs=(
            P("pb", "blk", None),
            P("pb", "blk", None, None),
            P("pb", "blk", None, None),
            P("pb", "blk"),
        ),
        check_vma=False,
    )
```

```python
import functools

import jax
import jax.numpy as jnp
import numpy as np
from jax import lax
from jax.experimental import pallas as pl
from jax.experimental.pallas import tpu as pltpu
from jax.sharding import PartitionSpec as P

HDIM = 64
PAIR = 2 * HDIM
SCORE_SCALE = 0.125
LOG2E = float(np.log2(np.e))
SCORE_LOG2 = SCORE_SCALE * LOG2E
NEGATIVE = -1e30
FACTORS = (8, 4, 2, 2)
VMEM_LIMIT = 24 * 1024 * 1024
VMEM_WIDE = 60 * 1024 * 1024
STAT_ROWS = 8


def cost(microseconds):
    return pl.CostEstimate(
        flops=int(1.1e9 * microseconds), bytes_accessed=1000, transcendentals=0
    )

NT = (((1,), (1,)), ((), ()))
NN = (((1,), (0,)), ((), ()))


def dot(lhs, rhs, dims):
    return lax.dot_general(lhs, rhs, dims, preferred_element_type=jnp.float32)


def head_masks():
    lane = lax.broadcasted_iota(jnp.int32, (1, PAIR), 1)
    first = (lane < HDIM).astype(jnp.float32)
    return first.astype(jnp.bfloat16), (1.0 - first).astype(jnp.bfloat16)


def by_head(rows):
    first, second = head_masks()
    return [rows * first, rows * second]


def valid_keys(lengths, passage_len, shape):
    token = lax.broadcasted_iota(jnp.int32, shape, 0)
    limit = jnp.full(shape, lengths[0], jnp.int32)
    for passage in range(1, len(lengths)):
        limit = jnp.where(
            token >= passage * passage_len, passage * passage_len + lengths[passage], limit
        )
    return token < limit


def local_stats(stacked, key_pair, lengths, passage_len):
    scores = dot(key_pair, stacked, NT) * SCORE_LOG2
    scores = jnp.where(valid_keys(lengths, passage_len, scores.shape), scores, NEGATIVE)
    row_max = jnp.max(scores, axis=0, keepdims=True)
    row_total = jnp.sum(jnp.exp2(scores - row_max), axis=0, keepdims=True)
    return row_max, row_total


def own_stats_kernel(pairs, passage_len, passages, len_ref, q_ref, k_ref, g_ref, o_ref, out_ref):
    lengths = [len_ref[i] for i in range(passages)]
    for j in range(pairs):
        cols = slice(j * PAIR, (j + 1) * PAIR)
        stacked = jnp.concatenate(by_head(q_ref[:, cols]), axis=0)
        row_max, row_total = local_stats(stacked, k_ref[:, cols], lengths, passage_len)
        product = g_ref[:, cols].astype(jnp.float32) * o_ref[:, cols].astype(jnp.float32)
        lane = lax.broadcasted_iota(jnp.int32, product.shape, 1)
        both = jnp.concatenate(
            [jnp.where(lane < HDIM, product, 0.0), jnp.where(lane < HDIM, 0.0, product)], axis=0
        )
        delta = jnp.sum(jnp.transpose(both), axis=0, keepdims=True)
        out_ref[j, 0:1, :] = row_max
        out_ref[j, 1:2, :] = row_total
        out_ref[j, 2:3, :] = delta
        out_ref[j, 3:STAT_ROWS, :] = jnp.zeros((STAT_ROWS - 3, row_max.shape[1]), jnp.float32)


def peer_stats_kernel(pairs, passage_len, passages, len_ref, q_ref, k_ref, own_ref, out_ref):
    lengths = [len_ref[i] for i in range(passages)]
    for j in range(pairs):
        cols = slice(j * PAIR, (j + 1) * PAIR)
        stacked = jnp.concatenate(by_head(q_ref[:, cols]), axis=0)
        row_max, row_total = local_stats(stacked, k_ref[:, cols], lengths, passage_len)
        out_ref[j] = own_ref[j]
        out_ref[j, 3:4, :] = row_max
        out_ref[j, 4:5, :] = row_total


def stats_call(kernel, lengths, key_rows, row_arrays, stat_arrays, passage_len, pairs):
    tokens, hd = key_rows.shape
    rows = row_arrays[0].shape[0]
    total_pairs = hd // PAIR
    wide = pairs * PAIR
    row_spec = pl.BlockSpec((rows, wide), lambda i, s: (0, i))
    key_spec = pl.BlockSpec((tokens, wide), lambda i, s: (0, i))
    stat_spec = pl.BlockSpec((pairs, STAT_ROWS, 2 * rows), lambda i, s: (i, 0, 0))
    return pl.pallas_call(
        functools.partial(kernel, pairs, passage_len, lengths.shape[0]),
        out_shape=jax.ShapeDtypeStruct((total_pairs, STAT_ROWS, 2 * rows), jnp.float32),
        grid_spec=pltpu.PrefetchScalarGridSpec(
            num_scalar_prefetch=1,
            grid=(total_pairs // pairs,),
            in_specs=[row_spec, key_spec]
            + [row_spec] * (len(row_arrays) - 1)
            + [stat_spec] * len(stat_arrays),
            out_specs=stat_spec,
        ),
        compiler_params=pltpu.CompilerParams(vmem_limit_bytes=VMEM_WIDE),
        cost_estimate=cost(3),
    )(lengths, row_arrays[0], key_rows, *row_arrays[1:], *stat_arrays)


def grad_kernel(
    pairs, passage_len, passages, carried, s_ref, mine_ref, theirs_ref, qo_ref, qp_ref, go_ref,
    gp_ref, k_ref, v_ref, *rest
):
    dq_ref, dk_ref, dv_ref = rest[2:] if carried else rest
    lengths = [s_ref[1 + i] for i in range(passages)]
    rows = qo_ref.shape[0]
    for j in range(pairs):
        cols = slice(j * PAIR, (j + 1) * PAIR)
        mine, theirs = mine_ref[j], theirs_ref[j]

        def log_total(first_max, first_total, second_max, second_total):
            top = jnp.maximum(first_max, second_max)
            total = first_total * jnp.exp2(first_max - top) + second_total * jnp.exp2(
                second_max - top
            )
            return top + jnp.log2(total)

        lse = jnp.concatenate(
            [
                log_total(mine[0:1], mine[1:2], theirs[3:4], theirs[4:5]),
                log_total(mine[3:4], mine[4:5], theirs[0:1], theirs[1:2]),
            ],
            axis=1,
        )
        delta = jnp.concatenate([mine[2:3], theirs[2:3]], axis=1)
        queries = jnp.concatenate(by_head(qo_ref[:, cols]) + by_head(qp_ref[:, cols]), axis=0)
        grads = jnp.concatenate(by_head(go_ref[:, cols]) + by_head(gp_ref[:, cols]), axis=0)
        key_pair = k_ref[:, cols]
        scores = dot(key_pair, queries, NT)
        probs = jnp.exp2(scores * SCORE_LOG2 - lse)
        probs = jnp.where(valid_keys(lengths, passage_len, scores.shape), probs, 0.0)
        dv_ref[:, cols] = dot(probs.astype(jnp.bfloat16), grads, NN).astype(jnp.bfloat16)
        prob_grad = dot(v_ref[:, cols], grads, NT)
        score_grad = (probs * (prob_grad - delta)).astype(jnp.bfloat16)
        dk_ref[:, cols] = (dot(score_grad, queries, NN) * SCORE_SCALE).astype(jnp.bfloat16)
        query_t = dot(jnp.transpose(key_pair), score_grad, NN) * SCORE_SCALE
        query_grad = jnp.transpose(query_t)
        lane = lax.broadcasted_iota(jnp.int32, (rows, PAIR), 1)
        for which in range(2):
            at = which * 2 * rows
            dq_ref[which if carried else 1 - which, :, cols] = jnp.where(
                lane < HDIM, query_grad[at : at + rows], query_grad[at + rows : at + 2 * rows]
            ).astype(dq_ref.dtype)


def grad_call(scalars, mine, theirs, rows4, key_rows, value_rows, carried, dq_type, passage_len,
              passages, pairs):
    tokens, hd = key_rows.shape
    rows = rows4[0].shape[0]
    half = hd // 2
    wide = pairs * PAIR
    steps = half // wide
    row_spec = pl.BlockSpec((rows, wide), lambda i, s: (0, s[0] * steps + i))
    key_spec = pl.BlockSpec((tokens, wide), lambda i, s: (0, s[0] * steps + i))
    stat_spec = pl.BlockSpec(
        (pairs, STAT_ROWS, 2 * rows), lambda i, s: (s[0] * steps + i, 0, 0)
    )
    any_spec = pl.BlockSpec(memory_space=pl.ANY)
    grad_shape = jax.ShapeDtypeStruct((tokens, hd), jnp.bfloat16)
    return pl.pallas_call(
        functools.partial(grad_kernel, pairs, passage_len, passages, len(carried) > 0),
        out_shape=(jax.ShapeDtypeStruct((2, rows, half), dq_type), grad_shape, grad_shape),
        grid_spec=pltpu.PrefetchScalarGridSpec(
            num_scalar_prefetch=1,
            grid=(steps,),
            in_specs=[stat_spec] * 2 + [row_spec] * 4 + [key_spec] * 2
            + [any_spec] * len(carried),
            out_specs=(
                pl.BlockSpec((2, rows, wide), lambda i, s: (0, 0, i)), key_spec, key_spec
            ),
        ),
        input_output_aliases={9: 1, 10: 2} if carried else {},
        compiler_params=pltpu.CompilerParams(vmem_limit_bytes=VMEM_WIDE),
        cost_estimate=cost(6),
    )(scalars, mine, theirs, *rows4, key_rows, value_rows, *carried)


def whole(shape):
    return pl.BlockSpec(shape, lambda i, s: (0,) * len(shape))


def weight_kernel(chunk, part, s_ref, own_ref, peer_ref, *rest):
    blocks, (kept_ref, given_ref), term_ref = rest[:-3], rest[-3:-1], rest[-1]
    core, x_at = s_ref[0], s_ref[1]
    tokens = jnp.concatenate(
        [ref[y] for y in range(len(blocks)) for ref in (own_ref, peer_ref)], axis=0
    )
    term_ref[...] = dot(
        jnp.transpose(tokens), jnp.concatenate([ref[...] for ref in blocks], axis=0), NN
    )
    cores = 2
    per_z = 2 * cores * part
    for z in range(chunk // per_z):
        for x in range(2):
            base = z * per_z + (x_at ^ x) * (cores * part)
            kept_ref[x, z] = term_ref[pl.ds(pl.multiple_of(base + core * part, part), part), :]
            given_ref[x, z] = term_ref[
                pl.ds(pl.multiple_of(base + (1 - core) * part, part), part), :
            ].astype(jnp.bfloat16)


def weight_call(scalars, hidden_own, hidden_peer, blocks, nz, part, z_step):
    ny, rows, tile = hidden_own.shape
    features = blocks[0].shape[1]
    chunk = z_step * 4 * part
    hidden_spec = pl.BlockSpec((ny, rows, chunk), lambda i, s: (0, 0, i))
    out_spec = pl.BlockSpec((2, z_step, part, features), lambda i, s: (0, i, 0, 0))
    shape = (2, nz, part, features)
    return pl.pallas_call(
        functools.partial(weight_kernel, chunk, part),
        out_shape=(
            jax.ShapeDtypeStruct(shape, jnp.float32), jax.ShapeDtypeStruct(shape, jnp.bfloat16)
        ),
        grid_spec=pltpu.PrefetchScalarGridSpec(
            num_scalar_prefetch=1,
            grid=(nz // z_step,),
            in_specs=[hidden_spec] * 2 + [whole(blocks[0].shape)] * ny,
            out_specs=(out_spec, out_spec),
            scratch_shapes=[pltpu.VMEM((chunk, features), jnp.float32)],
        ),
        compiler_params=pltpu.CompilerParams(vmem_limit_bytes=VMEM_LIMIT),
        cost_estimate=cost(2),
    )(scalars, hidden_own, hidden_peer, *blocks)


def state_kernel(rows, s_ref, w_ref, *rest):
    blocks, (kept_ref, given_ref) = rest[:-2], rest[-2:]
    term = dot(jnp.concatenate([ref[...] for ref in blocks], axis=0), w_ref[...], NT)
    for y in range(len(blocks)):
        at = y * 2 * rows
        kept_ref[y] = term[at : at + rows]
        given_ref[y] = term[at + rows : at + 2 * rows].astype(jnp.bfloat16)


def state_call(scalars, w_tile, blocks, chunk):
    ny, tile, features = len(blocks), w_tile.shape[0], w_tile.shape[1]
    rows = blocks[0].shape[0] // 2
    out_spec = pl.BlockSpec((ny, rows, chunk), lambda i, s: (0, 0, i))
    shape = (ny, rows, tile)
    return pl.pallas_call(
        functools.partial(state_kernel, rows),
        out_shape=(
            jax.ShapeDtypeStruct(shape, jnp.float32), jax.ShapeDtypeStruct(shape, jnp.bfloat16)
        ),
        grid_spec=pltpu.PrefetchScalarGridSpec(
            num_scalar_prefetch=1,
            grid=(tile // chunk,),
            in_specs=[pl.BlockSpec((chunk, features), lambda i, s: (i, 0))]
            + [whole(blocks[0].shape)] * ny,
            out_specs=(out_spec, out_spec),
        ),
        compiler_params=pltpu.CompilerParams(vmem_limit_bytes=VMEM_LIMIT),
        cost_estimate=cost(2),
    )(scalars, w_tile, *blocks)


def split_kernel(nz, s_ref, in_ref, *out_refs):
    ny = len(out_refs)
    width = in_ref.shape[1] // (nz * ny)
    for offset, out_ref in enumerate(out_refs):
        owner = lax.rem(s_ref[2] + (ny - offset), ny)
        for z in range(nz):
            at = pl.multiple_of((z * ny + owner) * width, width)
            out_ref[:, z * width : (z + 1) * width] = in_ref[:, pl.ds(at, width)]


def split_call(scalars, array, nz, ny):
    rows, width = array.shape
    shape = (rows, width // ny)
    return pl.pallas_call(
        functools.partial(split_kernel, nz),
        out_shape=[jax.ShapeDtypeStruct(shape, array.dtype)] * ny,
        grid_spec=pltpu.PrefetchScalarGridSpec(
            num_scalar_prefetch=1,
            grid=(1,),
            in_specs=[whole(array.shape)],
            out_specs=[whole(shape)] * ny,
        ),
        compiler_params=pltpu.CompilerParams(vmem_limit_bytes=VMEM_LIMIT),
        cost_estimate=cost(1),
    )(scalars, array)


def place_kernel(nz, s_ref, *rest):
    blocks, out_ref = rest[:-1], rest[-1]
    ny = len(blocks)
    width = blocks[0].shape[1] // nz
    for offset, block in enumerate(blocks):
        owner = lax.rem(s_ref[2] + (ny - offset), ny)
        for z in range(nz):
            at = pl.multiple_of((z * ny + owner) * width, width)
            out_ref[:, pl.ds(at, width)] = block[:, z * width : (z + 1) * width]


def place_call(scalars, blocks, nz):
    rows, tile = blocks[0].shape
    shape = (rows, tile * len(blocks))
    return pl.pallas_call(
        functools.partial(place_kernel, nz),
        out_shape=jax.ShapeDtypeStruct(shape, blocks[0].dtype),
        grid_spec=pltpu.PrefetchScalarGridSpec(
            num_scalar_prefetch=1,
            grid=(1,),
            in_specs=[whole((rows, tile))] * len(blocks),
            out_specs=whole(shape),
        ),
        compiler_params=pltpu.CompilerParams(vmem_limit_bytes=VMEM_LIMIT),
        cost_estimate=cost(1),
    )(scalars, *blocks)


def on_device(hidden, query, out_grad, attn_out, keys, values, lengths, w_query):
    nz, ny, nx, nc = FACTORS
    plane = ny * nx * nc
    devices = nz * plane
    blk, pb = lax.axis_index("blk"), lax.axis_index("pb")
    core, x_at = lax.rem(pb, nc), lax.rem(pb // nc, nx)
    y_at = lax.rem(pb // (nx * nc), ny)
    offsets = list(dict.fromkeys((1, ny - 1, *range(2, ny - 1))))
    place = jnp.stack([core, x_at, y_at]).astype(jnp.int32)
    z_groups = [[z * plane + r for z in range(nz)] for r in range(plane)]

    def other_blk(x):
        return lax.ppermute(x, "blk", [(0, 1), (1, 0)])

    def other_core(x):
        return lax.ppermute(x, "pb", [(i, i ^ 1) for i in range(devices)])

    def other_x(x):
        return lax.ppermute(x, "pb", [(i, i ^ nc) for i in range(devices)])

    def from_y(x, offset):
        step = nx * nc
        def target(i):
            y = i // step % ny
            return i + ((y - offset) % ny - y) * step
        return lax.ppermute(x, "pb", [(i, target(i)) for i in range(devices)])

    tokens = keys.shape[1] * keys.shape[2]
    passages, passage_len = keys.shape[1], keys.shape[2]
    hd = keys.shape[3]
    rows, width = hidden.shape[1], hidden.shape[2]
    part = w_query.shape[0]
    key_rows, value_rows = keys.reshape(tokens, hd), values.reshape(tokens, hd)
    q_own, g_own, o_own = query[0], out_grad[0], attn_out[0]

    q_peer = other_blk(q_own)
    g_peer = other_blk(g_own)

    def in_order(first, mine, other):
        return jnp.where(
            first, jnp.concatenate([mine, other], axis=0), jnp.concatenate([other, mine], axis=0)
        )

    w_pair = in_order(core == 0, w_query, other_core(w_query))
    w_near = in_order(x_at == 0, w_pair, other_x(w_pair))
    w_tile = lax.all_gather(w_near, "pb", axis=0, tiled=True, axis_index_groups=z_groups)

    lens = lengths[0]
    stat_pairs = min(4, hd // PAIR)
    stats_own = stats_call(
        own_stats_kernel, lens, key_rows, [q_own, g_own, o_own], [], passage_len, stat_pairs
    )
    mine = stats_call(
        peer_stats_kernel, lens, key_rows, [q_peer], [stats_own], passage_len, stat_pairs
    )
    theirs = other_blk(mine)

    place, _ = lax.optimization_barrier((place, stats_own))
    shares = split_call(place, hidden[0], nz, ny)
    hidden_own = jnp.stack([shares[0]] + [from_y(shares[s], s) for s in offsets], axis=0)
    theirs, hidden_own = lax.optimization_barrier((theirs, hidden_own))

    rows4 = [q_own, q_peer, g_own, g_peer]
    grad_pairs = min(2, hd // PAIR // 2)

    def half_grad(which, carried, dq_type):
        scalars = jnp.concatenate([jnp.reshape(which, (1,)), lens]).astype(jnp.int32)
        return grad_call(scalars, mine, theirs, rows4, key_rows, value_rows, carried, dq_type,
                         passage_len, passages, grad_pairs)

    dq_send, key_part, value_part = half_grad(1 - blk, (), jnp.bfloat16)
    dq_here, key_grad, value_grad = half_grad(blk, (key_part, value_part), jnp.float32)
    dq_there = other_blk(dq_send)
    dq_there, dq_here, hidden_own = lax.optimization_barrier((dq_there, dq_here, hidden_own))
    hidden_peer = other_blk(hidden_own)
    qg = (dq_here + dq_there.astype(jnp.float32)).astype(jnp.bfloat16)
    qg = qg.reshape(2 * rows, hd // 2)

    blocks = [qg] + [from_y(qg, s) for s in offsets]

    w_kept, w_given = weight_call(place, hidden_own, hidden_peer, blocks, nz, part, max(nz // 4, 1))
    w_other = other_core(w_given)
    w_send = (w_kept[1] + w_other[1].astype(jnp.float32)).astype(jnp.bfloat16)
    w_sum = (w_kept[0] + w_other[0].astype(jnp.float32)) + other_x(w_send).astype(jnp.float32)
    w_parts = lax.all_to_all(
        w_sum.astype(jnp.bfloat16), "pb", split_axis=0, concat_axis=0, tiled=True,
        axis_index_groups=z_groups,
    )
    w_query_grad = jnp.sum(w_parts.astype(jnp.float32), axis=0)

    state_kept, state_given = state_call(place, w_tile, blocks, w_tile.shape[0] // 4)
    state_sum = (state_kept + other_blk(state_given).astype(jnp.float32)).astype(jnp.bfloat16)
    back = [state_sum[0]] + [None] * (ny - 1)
    for at, offset in enumerate(offsets):
        back[offset] = from_y(state_sum[at + 1], -offset)
    hidden_grad = place_call(place, back, nz).reshape(hidden.shape)
    return (hidden_grad, key_grad.reshape(keys.shape), value_grad.reshape(values.shape),
            w_query_grad)


def solution(mesh):
    return jax.shard_map(
        on_device,
        mesh=mesh,
        in_specs=(
            P("pb", "blk", None),
            P("pb", "blk", None),
            P("pb", "blk", None),
            P("pb", "blk", None),
            P("pb", "blk", None, None),
            P("pb", "blk", None, None),
            P("pb", "blk"),
            P("pb", "blk"),
        ),
        out_specs=(
            P("pb", "blk", None),
            P("pb", "blk", None, None),
            P("pb", "blk", None, None),
            P("pb", "blk"),
        ),
        check_vma=False,
    )
```

```python
import functools

import jax
import jax.numpy as jnp
import numpy as np
from jax import lax
from jax.experimental import pallas as pl
from jax.experimental.pallas import tpu as pltpu
from jax.sharding import PartitionSpec as P

HDIM = 64
PAIR = 2 * HDIM
SCORE_SCALE = 0.125
LOG2E = float(np.log2(np.e))
SCORE_LOG2 = SCORE_SCALE * LOG2E
NEGATIVE = -1e30
FACTORS = (8, 4, 2, 2)
VMEM_LIMIT = 16 * 1024 * 1024
VMEM_WIDE = 56 * 1024 * 1024
STAT_ROWS = 8


def cost(microseconds):
    return pl.CostEstimate(
        flops=int(1.1e9 * microseconds), bytes_accessed=1000, transcendentals=0
    )

NT = (((1,), (1,)), ((), ()))
NN = (((1,), (0,)), ((), ()))


def dot(lhs, rhs, dims):
    return lax.dot_general(lhs, rhs, dims, preferred_element_type=jnp.float32)


def head_masks():
    lane = lax.broadcasted_iota(jnp.int32, (1, PAIR), 1)
    first = (lane < HDIM).astype(jnp.float32)
    return first.astype(jnp.bfloat16), (1.0 - first).astype(jnp.bfloat16)


def by_head(rows):
    first, second = head_masks()
    return [rows * first, rows * second]


def valid_keys(lengths, passage_len, shape):
    token = lax.broadcasted_iota(jnp.int32, shape, 0)
    limit = jnp.full(shape, lengths[0], jnp.int32)
    for passage in range(1, len(lengths)):
        limit = jnp.where(
            token >= passage * passage_len, passage * passage_len + lengths[passage], limit
        )
    return token < limit


def local_stats(stacked, key_pair, lengths, passage_len):
    scores = dot(key_pair, stacked, NT) * SCORE_LOG2
    scores = jnp.where(valid_keys(lengths, passage_len, scores.shape), scores, NEGATIVE)
    row_max = jnp.max(scores, axis=0, keepdims=True)
    row_total = jnp.sum(jnp.exp2(scores - row_max), axis=0, keepdims=True)
    return row_max, row_total


def own_stats_kernel(pairs, passage_len, passages, len_ref, q_ref, k_ref, g_ref, o_ref, out_ref):
    lengths = [len_ref[i] for i in range(passages)]
    for j in range(pairs):
        cols = slice(j * PAIR, (j + 1) * PAIR)
        stacked = jnp.concatenate(by_head(q_ref[:, cols]), axis=0)
        row_max, row_total = local_stats(stacked, k_ref[:, cols], lengths, passage_len)
        product = g_ref[:, cols].astype(jnp.float32) * o_ref[:, cols].astype(jnp.float32)
        lane = lax.broadcasted_iota(jnp.int32, product.shape, 1)
        both = jnp.concatenate(
            [jnp.where(lane < HDIM, product, 0.0), jnp.where(lane < HDIM, 0.0, product)], axis=0
        )
        delta = jnp.sum(jnp.transpose(both), axis=0, keepdims=True)
        out_ref[j, 0:1, :] = row_max
        out_ref[j, 1:2, :] = row_total
        out_ref[j, 2:3, :] = delta
        out_ref[j, 3:STAT_ROWS, :] = jnp.zeros((STAT_ROWS - 3, row_max.shape[1]), jnp.float32)


def peer_stats_kernel(pairs, passage_len, passages, len_ref, q_ref, k_ref, own_ref, out_ref):
    lengths = [len_ref[i] for i in range(passages)]
    for j in range(pairs):
        cols = slice(j * PAIR, (j + 1) * PAIR)
        stacked = jnp.concatenate(by_head(q_ref[:, cols]), axis=0)
        row_max, row_total = local_stats(stacked, k_ref[:, cols], lengths, passage_len)
        out_ref[j] = own_ref[j]
        out_ref[j, 3:4, :] = row_max
        out_ref[j, 4:5, :] = row_total


def stats_call(kernel, vmem, lengths, key_rows, row_arrays, stat_arrays, passage_len, pairs):
    tokens, hd = key_rows.shape
    rows = row_arrays[0].shape[0]
    total_pairs = hd // PAIR
    wide = pairs * PAIR
    row_spec = pl.BlockSpec((rows, wide), lambda i, s: (0, i))
    key_spec = pl.BlockSpec((tokens, wide), lambda i, s: (0, i))
    stat_spec = pl.BlockSpec((pairs, STAT_ROWS, 2 * rows), lambda i, s: (i, 0, 0))
    return pl.pallas_call(
        functools.partial(kernel, pairs, passage_len, lengths.shape[0]),
        out_shape=jax.ShapeDtypeStruct((total_pairs, STAT_ROWS, 2 * rows), jnp.float32),
        grid_spec=pltpu.PrefetchScalarGridSpec(
            num_scalar_prefetch=1,
            grid=(total_pairs // pairs,),
            in_specs=[row_spec, key_spec]
            + [row_spec] * (len(row_arrays) - 1)
            + [stat_spec] * len(stat_arrays),
            out_specs=stat_spec,
        ),
        compiler_params=pltpu.CompilerParams(vmem_limit_bytes=vmem),
        cost_estimate=cost(3),
    )(lengths, row_arrays[0], key_rows, *row_arrays[1:], *stat_arrays)


def grad_kernel(
    pairs, passage_len, passages, carried, s_ref, mine_ref, theirs_ref, qo_ref, qp_ref, go_ref,
    gp_ref, k_ref, v_ref, *rest
):
    dq_ref, dk_ref, dv_ref = rest[2:] if carried else rest
    lengths = [s_ref[1 + i] for i in range(passages)]
    rows = qo_ref.shape[0]
    for j in range(pairs):
        cols = slice(j * PAIR, (j + 1) * PAIR)
        mine, theirs = mine_ref[j], theirs_ref[j]

        def log_total(first_max, first_total, second_max, second_total):
            top = jnp.maximum(first_max, second_max)
            total = first_total * jnp.exp2(first_max - top) + second_total * jnp.exp2(
                second_max - top
            )
            return top + jnp.log2(total)

        lse = jnp.concatenate(
            [
                log_total(mine[0:1], mine[1:2], theirs[3:4], theirs[4:5]),
                log_total(mine[3:4], mine[4:5], theirs[0:1], theirs[1:2]),
            ],
            axis=1,
        )
        delta = jnp.concatenate([mine[2:3], theirs[2:3]], axis=1)
        queries = jnp.concatenate(by_head(qo_ref[:, cols]) + by_head(qp_ref[:, cols]), axis=0)
        grads = jnp.concatenate(by_head(go_ref[:, cols]) + by_head(gp_ref[:, cols]), axis=0)
        key_pair = k_ref[:, cols]
        scores = dot(key_pair, queries, NT)
        probs = jnp.exp2(scores * SCORE_LOG2 - lse)
        probs = jnp.where(valid_keys(lengths, passage_len, scores.shape), probs, 0.0)
        dv_ref[:, cols] = dot(probs.astype(jnp.bfloat16), grads, NN).astype(jnp.bfloat16)
        prob_grad = dot(v_ref[:, cols], grads, NT)
        score_grad = (probs * (prob_grad - delta)).astype(jnp.bfloat16)
        dk_ref[:, cols] = (dot(score_grad, queries, NN) * SCORE_SCALE).astype(jnp.bfloat16)
        query_t = dot(jnp.transpose(key_pair), score_grad, NN) * SCORE_SCALE
        query_grad = jnp.transpose(query_t)
        lane = lax.broadcasted_iota(jnp.int32, (rows, PAIR), 1)
        for which in range(2):
            at = which * 2 * rows
            dq_ref[which if carried else 1 - which, :, cols] = jnp.where(
                lane < HDIM, query_grad[at : at + rows], query_grad[at + rows : at + 2 * rows]
            ).astype(dq_ref.dtype)


def grad_call(scalars, mine, theirs, rows4, key_rows, value_rows, carried, dq_type, passage_len,
              passages, pairs):
    tokens, hd = key_rows.shape
    rows = rows4[0].shape[0]
    half = hd // 2
    wide = pairs * PAIR
    steps = half // wide
    row_spec = pl.BlockSpec((rows, wide), lambda i, s: (0, s[0] * steps + i))
    key_spec = pl.BlockSpec((tokens, wide), lambda i, s: (0, s[0] * steps + i))
    stat_spec = pl.BlockSpec(
        (pairs, STAT_ROWS, 2 * rows), lambda i, s: (s[0] * steps + i, 0, 0)
    )
    any_spec = pl.BlockSpec(memory_space=pl.ANY)
    grad_shape = jax.ShapeDtypeStruct((tokens, hd), jnp.bfloat16)
    return pl.pallas_call(
        functools.partial(grad_kernel, pairs, passage_len, passages, len(carried) > 0),
        out_shape=(jax.ShapeDtypeStruct((2, rows, half), dq_type), grad_shape, grad_shape),
        grid_spec=pltpu.PrefetchScalarGridSpec(
            num_scalar_prefetch=1,
            grid=(steps,),
            in_specs=[stat_spec] * 2 + [row_spec] * 4 + [key_spec] * 2
            + [any_spec] * len(carried),
            out_specs=(
                pl.BlockSpec((2, rows, wide), lambda i, s: (0, 0, i)), key_spec, key_spec
            ),
        ),
        input_output_aliases={9: 1, 10: 2} if carried else {},
        compiler_params=pltpu.CompilerParams(vmem_limit_bytes=VMEM_WIDE),
        cost_estimate=cost(0.2 if carried else 6),
    )(scalars, mine, theirs, *rows4, key_rows, value_rows, *carried)


def whole(shape):
    return pl.BlockSpec(shape, lambda i, s: (0,) * len(shape))


def weight_kernel(chunk, part, s_ref, own_ref, peer_ref, *rest):
    blocks, (kept_ref, given_ref, all_ref, term_ref) = rest[:-4], rest[-4:]
    core, x_at, y_at = s_ref[0], s_ref[1], s_ref[2]
    tokens = jnp.concatenate(
        [
            ref[lax.rem(y_at + y, len(blocks))]
            for y in range(len(blocks))
            for ref in (own_ref, peer_ref)
        ],
        axis=0,
    )

    @pl.when(pl.program_id(0) == 0)
    def _():
        all_ref[...] = jnp.concatenate([ref[...] for ref in blocks], axis=0)

    term_ref[...] = dot(jnp.transpose(tokens), all_ref[...], NN)
    cores = 2
    per_z = 2 * cores * part
    for z in range(chunk // per_z):
        for x in range(2):
            base = z * per_z + (x_at ^ x) * (cores * part)
            kept_ref[x, z] = term_ref[pl.ds(pl.multiple_of(base + core * part, part), part), :]
            given_ref[x, z] = term_ref[
                pl.ds(pl.multiple_of(base + (1 - core) * part, part), part), :
            ].astype(jnp.bfloat16)


def weight_call(scalars, hidden_own, hidden_peer, blocks, nz, part, z_step):
    ny, rows, tile = hidden_own.shape
    features = blocks[0].shape[1]
    chunk = z_step * 4 * part
    hidden_spec = pl.BlockSpec((ny, rows, chunk), lambda i, s: (0, 0, i))
    out_spec = pl.BlockSpec((2, z_step, part, features), lambda i, s: (0, i, 0, 0))
    shape = (2, nz, part, features)
    return pl.pallas_call(
        functools.partial(weight_kernel, chunk, part),
        out_shape=(
            jax.ShapeDtypeStruct(shape, jnp.float32),
            jax.ShapeDtypeStruct(shape, jnp.bfloat16),
            jax.ShapeDtypeStruct((ny * 2 * rows, features), jnp.bfloat16),
        ),
        grid_spec=pltpu.PrefetchScalarGridSpec(
            num_scalar_prefetch=1,
            grid=(nz // z_step,),
            in_specs=[hidden_spec] * 2 + [whole(blocks[0].shape)] * ny,
            out_specs=(out_spec, out_spec, whole((ny * 2 * rows, features))),
            scratch_shapes=[pltpu.VMEM((chunk, features), jnp.float32)],
        ),
        compiler_params=pltpu.CompilerParams(vmem_limit_bytes=VMEM_LIMIT),
        cost_estimate=cost(2),
    )(scalars, hidden_own, hidden_peer, *blocks)


def state_kernel(rows, s_ref, mine_ref, other_ref, all_ref, kept_ref, given_ref):
    first = s_ref[0] == 0
    nz, near, _ = mine_ref.shape
    part = near // 2
    weight = []
    for z in range(nz):
        for x in range(2):
            mine = mine_ref[z, x * part : (x + 1) * part]
            other = other_ref[z, x * part : (x + 1) * part]
            weight += [jnp.where(first, mine, other), jnp.where(first, other, mine)]
    term = dot(all_ref[...], jnp.concatenate(weight, axis=0), NT)
    for y in range(kept_ref.shape[0]):
        at = y * 2 * rows
        kept_ref[y] = term[at : at + rows]
        given_ref[y] = term[at + rows : at + 2 * rows].astype(jnp.bfloat16)


def state_call(scalars, w_mine, w_sibling, tokens, rows, z_step):
    ny, (nz, near, features) = tokens.shape[0] // (2 * rows), w_mine.shape
    chunk = z_step * near * 2
    w_spec = pl.BlockSpec((z_step, near, features), lambda i, s: (i, 0, 0))
    out_spec = pl.BlockSpec((ny, rows, chunk), lambda i, s: (0, 0, i))
    shape = (ny, rows, nz * near * 2)
    return pl.pallas_call(
        functools.partial(state_kernel, rows),
        out_shape=(
            jax.ShapeDtypeStruct(shape, jnp.float32), jax.ShapeDtypeStruct(shape, jnp.bfloat16)
        ),
        grid_spec=pltpu.PrefetchScalarGridSpec(
            num_scalar_prefetch=1,
            grid=(nz // z_step,),
            in_specs=[w_spec] * 2 + [whole(tokens.shape)],
            out_specs=(out_spec, out_spec),
        ),
        compiler_params=pltpu.CompilerParams(vmem_limit_bytes=VMEM_LIMIT),
        cost_estimate=cost(2),
    )(scalars, w_mine, w_sibling, tokens)


def split_kernel(in_ref, out_ref):
    ny, _, tile = out_ref.shape
    width = PAIR
    for y in range(ny):
        for z in range(tile // width):
            at = (z * ny + y) * width
            out_ref[y, :, z * width : (z + 1) * width] = in_ref[:, at : at + width]


def split_call(array, ny):
    rows, width = array.shape
    return pl.pallas_call(
        split_kernel,
        out_shape=jax.ShapeDtypeStruct((ny, rows, width // ny), array.dtype),
        compiler_params=pltpu.CompilerParams(vmem_limit_bytes=VMEM_LIMIT),
        cost_estimate=cost(1),
    )(array)


def place_kernel(z_order, s_ref, *rest):
    blocks, out_ref = rest[:-1], rest[-1]
    ny, width = len(blocks), PAIR
    for offset, block in enumerate(blocks):
        owner = lax.rem(s_ref[2] + (ny - offset), ny)
        for z, flip in enumerate(z_order):
            at = pl.multiple_of(((s_ref[3] ^ flip) * ny + owner) * width, width)
            out_ref[:, pl.ds(at, width)] = block[:, z * width : (z + 1) * width]


def place_call(scalars, blocks, z_order):
    rows, tile = blocks[0].shape
    shape = (rows, tile * len(blocks))
    return pl.pallas_call(
        functools.partial(place_kernel, z_order),
        out_shape=jax.ShapeDtypeStruct(shape, blocks[0].dtype),
        grid_spec=pltpu.PrefetchScalarGridSpec(
            num_scalar_prefetch=1,
            grid=(1,),
            in_specs=[whole((rows, tile))] * len(blocks),
            out_specs=whole(shape),
        ),
        compiler_params=pltpu.CompilerParams(vmem_limit_bytes=VMEM_LIMIT),
        cost_estimate=cost(1),
    )(scalars, *blocks)


def on_device(hidden, query, out_grad, attn_out, keys, values, lengths, w_query):
    nz, ny, nx, nc = FACTORS
    plane = ny * nx * nc
    devices = nz * plane
    blk, pb = lax.axis_index("blk"), lax.axis_index("pb")
    core, x_at = lax.rem(pb, nc), lax.rem(pb // nc, nx)
    y_at = lax.rem(pb // (nx * nc), ny)
    offsets = list(dict.fromkeys((1, ny - 1, *range(2, ny - 1))))
    z_at = pb // plane
    place = jnp.stack([core, x_at, y_at, z_at]).astype(jnp.int32)
    y_groups = [
        [z * plane + y * nx * nc + r for y in range(ny)] for z in range(nz) for r in range(nx * nc)
    ]
    z_groups = [[z * plane + r for z in range(nz)] for r in range(plane)]

    def other_blk(x):
        return lax.ppermute(x, "blk", [(0, 1), (1, 0)])

    def other_core(x):
        return lax.ppermute(x, "pb", [(i, i ^ 1) for i in range(devices)])

    def other_x(x):
        return lax.ppermute(x, "pb", [(i, i ^ nc) for i in range(devices)])

    def from_y(x, offset):
        step = nx * nc
        def target(i):
            y = i // step % ny
            return i + ((y - offset) % ny - y) * step
        return lax.ppermute(x, "pb", [(i, target(i)) for i in range(devices)])

    def other_z(x, flip):
        return lax.ppermute(x, "pb", [(i, i ^ (flip * plane)) for i in range(devices)])

    def swap_y(x):
        return lax.all_to_all(
            x, "pb", split_axis=0, concat_axis=0, tiled=True, axis_index_groups=y_groups
        )

    def swap_z(x):
        return lax.all_to_all(
            x, "pb", split_axis=0, concat_axis=0, tiled=True, axis_index_groups=z_groups
        )

    def after(x, *others):
        return lax.optimization_barrier((x, *others))[0]

    tokens = keys.shape[1] * keys.shape[2]
    passages, passage_len = keys.shape[1], keys.shape[2]
    hd = keys.shape[3]
    rows, width = hidden.shape[1], hidden.shape[2]
    part = w_query.shape[0]
    key_rows, value_rows = keys.reshape(tokens, hd), values.reshape(tokens, hd)
    q_own, g_own, o_own = query[0], out_grad[0], attn_out[0]

    q_peer = other_blk(q_own)
    g_peer = other_blk(g_own)

    lens = lengths[0]
    stat_pairs = min(4, hd // PAIR)
    stats_own = stats_call(
        own_stats_kernel, VMEM_WIDE, lens, key_rows, [q_own, g_own, o_own], [], passage_len, stat_pairs
    )
    w_there = other_x(w_query)
    w_near = jnp.where(
        x_at == 0,
        jnp.concatenate([w_query, w_there], axis=0),
        jnp.concatenate([w_there, w_query], axis=0),
    )
    mine = stats_call(
        peer_stats_kernel, VMEM_LIMIT, lens, key_rows, [q_peer], [stats_own], passage_len, stat_pairs
    )
    theirs = other_blk(mine)

    shares = split_call(hidden[0], ny)
    hidden_own = swap_y(after(shares, mine))

    w_mine, flip, z_order = after(w_near, mine)[None], nz // 2, [0]

    def along_z(w_rows, flip, order):
        if flip == 0:
            return w_rows, order
        return jnp.concatenate([w_rows, other_z(w_rows, flip)], axis=0), order + [
            z ^ flip for z in order
        ]

    w_mine, z_order = along_z(w_mine, flip, z_order)

    rows4 = [q_own, q_peer, g_own, g_peer]
    grad_pairs = min(2, hd // PAIR // 2)

    def half_grad(which, carried, dq_type):
        scalars = jnp.concatenate([jnp.reshape(which, (1,)), lens]).astype(jnp.int32)
        return grad_call(scalars, mine, theirs, rows4, key_rows, value_rows, carried, dq_type,
                         passage_len, passages, grad_pairs)

    dq_send, key_part, value_part = half_grad(1 - blk, (), jnp.bfloat16)
    lens = after(lens, w_mine)
    dq_here, key_grad, value_grad = half_grad(blk, (key_part, value_part), jnp.float32)
    dq_there = other_blk(dq_send)
    dq_there, dq_here, hidden_own = lax.optimization_barrier((dq_there, dq_here, hidden_own))
    qg = (dq_here + dq_there.astype(jnp.float32)).astype(jnp.bfloat16)
    qg = qg.reshape(2 * rows, hd // 2)
    hidden_peer = other_blk(hidden_own)

    arrived = {s: from_y(qg, s) for s in offsets}
    blocks = [qg] + [arrived[s] for s in range(1, ny)]

    w_mine, z_order = along_z(w_mine, flip // 2, z_order)

    w_kept, w_given, qg_all = weight_call(
        after(place, w_mine), hidden_own, hidden_peer, blocks, nz, part, max(nz // 4, 1)
    )
    w_other = other_core(w_given)
    w_send = (w_kept[1] + w_other[1].astype(jnp.float32)).astype(jnp.bfloat16)
    w_across = other_x(w_send)
    w_sum = (w_kept[0] + w_other[0].astype(jnp.float32)) + w_across.astype(jnp.float32)

    w_mine, z_order = along_z(after(w_mine, w_send), flip // 4, z_order)
    w_sibling = other_core(after(w_mine, w_across))
    state_kept, state_given = state_call(
        place, w_mine, w_sibling, qg_all, rows, max(nz // 4, 1)
    )
    state_there = other_blk(state_given)
    w_parts = swap_z(w_sum.astype(jnp.bfloat16))
    w_query_grad = jnp.sum(w_parts.astype(jnp.float32), axis=0)
    state_sum = (state_kept + state_there.astype(jnp.float32)).astype(jnp.bfloat16)
    back = [state_sum[0]] + [from_y(state_sum[s], -s) for s in range(1, ny)]
    hidden_grad = place_call(place, back, z_order).reshape(hidden.shape)
    return (hidden_grad, key_grad.reshape(keys.shape), value_grad.reshape(values.shape),
            w_query_grad)


def solution(mesh):
    return jax.shard_map(
        on_device,
        mesh=mesh,
        in_specs=(
            P("pb", "blk", None),
            P("pb", "blk", None),
            P("pb", "blk", None),
            P("pb", "blk", None),
            P("pb", "blk", None, None),
            P("pb", "blk", None, None),
            P("pb", "blk"),
            P("pb", "blk"),
        ),
        out_specs=(
            P("pb", "blk", None),
            P("pb", "blk", None, None),
            P("pb", "blk", None, None),
            P("pb", "blk"),
        ),
        check_vma=False,
    )
```

```python
import functools

import jax
import jax.numpy as jnp
import numpy as np
from jax import lax
from jax.experimental import pallas as pl
from jax.experimental.pallas import tpu as pltpu
from jax.sharding import PartitionSpec as P

HDIM = 64
PAIR = 2 * HDIM
SCORE_SCALE = 0.125
LOG2E = float(np.log2(np.e))
SCORE_LOG2 = SCORE_SCALE * LOG2E
NEGATIVE = -1e30
FACTORS = (8, 4, 2, 2)
VMEM_LIMIT = 16 * 1024 * 1024
VMEM_WIDE = 56 * 1024 * 1024
STAT_ROWS = 8


def cost(microseconds):
    return pl.CostEstimate(
        flops=int(1.1e9 * microseconds), bytes_accessed=1000, transcendentals=0
    )

NT = (((1,), (1,)), ((), ()))
NN = (((1,), (0,)), ((), ()))


def dot(lhs, rhs, dims):
    return lax.dot_general(lhs, rhs, dims, preferred_element_type=jnp.float32)


def head_masks():
    lane = lax.broadcasted_iota(jnp.int32, (1, PAIR), 1)
    first = (lane < HDIM).astype(jnp.float32)
    return first.astype(jnp.bfloat16), (1.0 - first).astype(jnp.bfloat16)


def by_head(rows):
    first, second = head_masks()
    return [rows * first, rows * second]


def valid_keys(lengths, passage_len, shape):
    token = lax.broadcasted_iota(jnp.int32, shape, 0)
    limit = jnp.full(shape, lengths[0], jnp.int32)
    for passage in range(1, len(lengths)):
        limit = jnp.where(
            token >= passage * passage_len, passage * passage_len + lengths[passage], limit
        )
    return token < limit


def local_stats(stacked, key_pair, lengths, passage_len):
    scores = dot(key_pair, stacked, NT) * SCORE_LOG2
    scores = jnp.where(valid_keys(lengths, passage_len, scores.shape), scores, NEGATIVE)
    row_max = jnp.max(scores, axis=0, keepdims=True)
    row_total = jnp.sum(jnp.exp2(scores - row_max), axis=0, keepdims=True)
    return row_max, row_total


def own_stats_kernel(pairs, passage_len, passages, len_ref, q_ref, k_ref, g_ref, o_ref, out_ref):
    lengths = [len_ref[i] for i in range(passages)]
    for j in range(pairs):
        cols = slice(j * PAIR, (j + 1) * PAIR)
        stacked = jnp.concatenate(by_head(q_ref[:, cols]), axis=0)
        row_max, row_total = local_stats(stacked, k_ref[:, cols], lengths, passage_len)
        product = g_ref[:, cols].astype(jnp.float32) * o_ref[:, cols].astype(jnp.float32)
        lane = lax.broadcasted_iota(jnp.int32, product.shape, 1)
        both = jnp.concatenate(
            [jnp.where(lane < HDIM, product, 0.0), jnp.where(lane < HDIM, 0.0, product)], axis=0
        )
        delta = jnp.sum(jnp.transpose(both), axis=0, keepdims=True)
        out_ref[j, 0:1, :] = row_max
        out_ref[j, 1:2, :] = row_total
        out_ref[j, 2:3, :] = delta
        out_ref[j, 3:STAT_ROWS, :] = jnp.zeros((STAT_ROWS - 3, row_max.shape[1]), jnp.float32)


def peer_stats_kernel(pairs, passage_len, passages, len_ref, q_ref, k_ref, own_ref, out_ref):
    lengths = [len_ref[i] for i in range(passages)]
    for j in range(pairs):
        cols = slice(j * PAIR, (j + 1) * PAIR)
        stacked = jnp.concatenate(by_head(q_ref[:, cols]), axis=0)
        row_max, row_total = local_stats(stacked, k_ref[:, cols], lengths, passage_len)
        out_ref[j] = own_ref[j]
        out_ref[j, 3:4, :] = row_max
        out_ref[j, 4:5, :] = row_total


def stats_call(kernel, vmem, lengths, key_rows, row_arrays, stat_arrays, passage_len, pairs):
    tokens, hd = key_rows.shape
    rows = row_arrays[0].shape[0]
    total_pairs = hd // PAIR
    wide = pairs * PAIR
    row_spec = pl.BlockSpec((rows, wide), lambda i, s: (0, i))
    key_spec = pl.BlockSpec((tokens, wide), lambda i, s: (0, i))
    stat_spec = pl.BlockSpec((pairs, STAT_ROWS, 2 * rows), lambda i, s: (i, 0, 0))
    return pl.pallas_call(
        functools.partial(kernel, pairs, passage_len, lengths.shape[0]),
        out_shape=jax.ShapeDtypeStruct((total_pairs, STAT_ROWS, 2 * rows), jnp.float32),
        grid_spec=pltpu.PrefetchScalarGridSpec(
            num_scalar_prefetch=1,
            grid=(total_pairs // pairs,),
            in_specs=[row_spec, key_spec]
            + [row_spec] * (len(row_arrays) - 1)
            + [stat_spec] * len(stat_arrays),
            out_specs=stat_spec,
        ),
        compiler_params=pltpu.CompilerParams(vmem_limit_bytes=vmem),
        cost_estimate=cost(3),
    )(lengths, row_arrays[0], key_rows, *row_arrays[1:], *stat_arrays)


def grad_kernel(
    pairs, passage_len, passages, carried, s_ref, mine_ref, theirs_ref, qo_ref, qp_ref, go_ref,
    gp_ref, k_ref, v_ref, *rest
):
    dq_ref, dk_ref, dv_ref = rest[2:] if carried else rest
    lengths = [s_ref[1 + i] for i in range(passages)]
    rows = qo_ref.shape[0]
    for j in range(pairs):
        cols = slice(j * PAIR, (j + 1) * PAIR)
        mine, theirs = mine_ref[j], theirs_ref[j]

        def log_total(first_max, first_total, second_max, second_total):
            top = jnp.maximum(first_max, second_max)
            total = first_total * jnp.exp2(first_max - top) + second_total * jnp.exp2(
                second_max - top
            )
            return top + jnp.log2(total)

        lse = jnp.concatenate(
            [
                log_total(mine[0:1], mine[1:2], theirs[3:4], theirs[4:5]),
                log_total(mine[3:4], mine[4:5], theirs[0:1], theirs[1:2]),
            ],
            axis=1,
        )
        delta = jnp.concatenate([mine[2:3], theirs[2:3]], axis=1)
        queries = jnp.concatenate(by_head(qo_ref[:, cols]) + by_head(qp_ref[:, cols]), axis=0)
        grads = jnp.concatenate(by_head(go_ref[:, cols]) + by_head(gp_ref[:, cols]), axis=0)
        key_pair = k_ref[:, cols]
        scores = dot(key_pair, queries, NT)
        probs = jnp.exp2(scores * SCORE_LOG2 - lse)
        probs = jnp.where(valid_keys(lengths, passage_len, scores.shape), probs, 0.0)
        dv_ref[:, cols] = dot(probs.astype(jnp.bfloat16), grads, NN).astype(jnp.bfloat16)
        prob_grad = dot(v_ref[:, cols], grads, NT)
        score_grad = (probs * (prob_grad - delta)).astype(jnp.bfloat16)
        dk_ref[:, cols] = (dot(score_grad, queries, NN) * SCORE_SCALE).astype(jnp.bfloat16)
        query_t = dot(jnp.transpose(key_pair), score_grad, NN) * SCORE_SCALE
        query_grad = jnp.transpose(query_t)
        lane = lax.broadcasted_iota(jnp.int32, (rows, PAIR), 1)
        for which in range(2):
            at = which * 2 * rows
            dq_ref[which if carried else 1 - which, :, cols] = jnp.where(
                lane < HDIM, query_grad[at : at + rows], query_grad[at + rows : at + 2 * rows]
            ).astype(dq_ref.dtype)


def grad_call(scalars, mine, theirs, rows4, key_rows, value_rows, carried, dq_type, passage_len,
              passages, pairs):
    tokens, hd = key_rows.shape
    rows = rows4[0].shape[0]
    half = hd // 2
    wide = pairs * PAIR
    steps = half // wide
    row_spec = pl.BlockSpec((rows, wide), lambda i, s: (0, s[0] * steps + i))
    key_spec = pl.BlockSpec((tokens, wide), lambda i, s: (0, s[0] * steps + i))
    stat_spec = pl.BlockSpec(
        (pairs, STAT_ROWS, 2 * rows), lambda i, s: (s[0] * steps + i, 0, 0)
    )
    any_spec = pl.BlockSpec(memory_space=pl.ANY)
    grad_shape = jax.ShapeDtypeStruct((tokens, hd), jnp.bfloat16)
    return pl.pallas_call(
        functools.partial(grad_kernel, pairs, passage_len, passages, len(carried) > 0),
        out_shape=(jax.ShapeDtypeStruct((2, rows, half), dq_type), grad_shape, grad_shape),
        grid_spec=pltpu.PrefetchScalarGridSpec(
            num_scalar_prefetch=1,
            grid=(steps,),
            in_specs=[stat_spec] * 2 + [row_spec] * 4 + [key_spec] * 2
            + [any_spec] * len(carried),
            out_specs=(
                pl.BlockSpec((2, rows, wide), lambda i, s: (0, 0, i)), key_spec, key_spec
            ),
        ),
        input_output_aliases={9: 1, 10: 2} if carried else {},
        compiler_params=pltpu.CompilerParams(vmem_limit_bytes=VMEM_WIDE),
        cost_estimate=cost(0.2 if carried else 6),
    )(scalars, mine, theirs, *rows4, key_rows, value_rows, *carried)


def whole(shape):
    return pl.BlockSpec(shape, lambda i, s: (0,) * len(shape))


def weight_kernel(chunk, part, s_ref, own_ref, peer_ref, *rest):
    blocks, (kept_ref, given_ref, all_ref, term_ref) = rest[:-4], rest[-4:]
    core, x_at, y_at = s_ref[0], s_ref[1], s_ref[2]
    tokens = jnp.concatenate(
        [
            ref[lax.rem(y_at + y, len(blocks))]
            for y in range(len(blocks))
            for ref in (own_ref, peer_ref)
        ],
        axis=0,
    )

    @pl.when(pl.program_id(0) == 0)
    def _():
        all_ref[...] = jnp.concatenate([ref[...] for ref in blocks], axis=0)

    term_ref[...] = dot(jnp.transpose(tokens), all_ref[...], NN)
    cores = 2
    per_z = 2 * cores * part
    for z in range(chunk // per_z):
        for x in range(2):
            base = z * per_z + (x_at ^ x) * (cores * part)
            kept_ref[x, z] = term_ref[pl.ds(pl.multiple_of(base + core * part, part), part), :]
            given_ref[x, z] = term_ref[
                pl.ds(pl.multiple_of(base + (1 - core) * part, part), part), :
            ].astype(jnp.bfloat16)


def weight_call(scalars, hidden_own, hidden_peer, blocks, nz, part, z_step):
    ny, rows, tile = hidden_own.shape
    features = blocks[0].shape[1]
    chunk = z_step * 4 * part
    hidden_spec = pl.BlockSpec((ny, rows, chunk), lambda i, s: (0, 0, i))
    out_spec = pl.BlockSpec((2, z_step, part, features), lambda i, s: (0, i, 0, 0))
    shape = (2, nz, part, features)
    return pl.pallas_call(
        functools.partial(weight_kernel, chunk, part),
        out_shape=(
            jax.ShapeDtypeStruct(shape, jnp.float32),
            jax.ShapeDtypeStruct(shape, jnp.bfloat16),
            jax.ShapeDtypeStruct((ny * 2 * rows, features), jnp.bfloat16),
        ),
        grid_spec=pltpu.PrefetchScalarGridSpec(
            num_scalar_prefetch=1,
            grid=(nz // z_step,),
            in_specs=[hidden_spec] * 2 + [whole(blocks[0].shape)] * ny,
            out_specs=(out_spec, out_spec, whole((ny * 2 * rows, features))),
            scratch_shapes=[pltpu.VMEM((chunk, features), jnp.float32)],
        ),
        compiler_params=pltpu.CompilerParams(vmem_limit_bytes=VMEM_LIMIT),
        cost_estimate=cost(2),
    )(scalars, hidden_own, hidden_peer, *blocks)


def state_kernel(rows, s_ref, mine_ref, other_ref, all_ref, kept_ref, given_ref):
    first = s_ref[0] == 0
    nz, near, _ = mine_ref.shape
    part = near // 2
    weight = []
    for z in range(nz):
        for x in range(2):
            mine = mine_ref[z, x * part : (x + 1) * part]
            other = other_ref[z, x * part : (x + 1) * part]
            weight += [jnp.where(first, mine, other), jnp.where(first, other, mine)]
    term = dot(all_ref[...], jnp.concatenate(weight, axis=0), NT)
    for y in range(kept_ref.shape[0]):
        at = y * 2 * rows
        kept_ref[y] = term[at : at + rows]
        given_ref[y] = term[at + rows : at + 2 * rows].astype(jnp.bfloat16)


def state_call(scalars, w_mine, w_sibling, tokens, rows, z_step):
    ny, (nz, near, features) = tokens.shape[0] // (2 * rows), w_mine.shape
    chunk = z_step * near * 2
    w_spec = pl.BlockSpec((z_step, near, features), lambda i, s: (i, 0, 0))
    out_spec = pl.BlockSpec((ny, rows, chunk), lambda i, s: (0, 0, i))
    shape = (ny, rows, nz * near * 2)
    return pl.pallas_call(
        functools.partial(state_kernel, rows),
        out_shape=(
            jax.ShapeDtypeStruct(shape, jnp.float32), jax.ShapeDtypeStruct(shape, jnp.bfloat16)
        ),
        grid_spec=pltpu.PrefetchScalarGridSpec(
            num_scalar_prefetch=1,
            grid=(nz // z_step,),
            in_specs=[w_spec] * 2 + [whole(tokens.shape)],
            out_specs=(out_spec, out_spec),
        ),
        compiler_params=pltpu.CompilerParams(vmem_limit_bytes=VMEM_LIMIT),
        cost_estimate=cost(2),
    )(scalars, w_mine, w_sibling, tokens)


def split_kernel(in_ref, out_ref):
    ny, _, tile = out_ref.shape
    width = PAIR
    for y in range(ny):
        for z in range(tile // width):
            at = (z * ny + y) * width
            out_ref[y, :, z * width : (z + 1) * width] = in_ref[:, at : at + width]


def split_call(array, ny):
    rows, width = array.shape
    return pl.pallas_call(
        split_kernel,
        out_shape=jax.ShapeDtypeStruct((ny, rows, width // ny), array.dtype),
        compiler_params=pltpu.CompilerParams(vmem_limit_bytes=VMEM_LIMIT),
        cost_estimate=cost(1),
    )(array)


def place_kernel(z_order, s_ref, *rest):
    blocks, out_ref = rest[:-1], rest[-1]
    ny, width = len(blocks), PAIR
    for offset, block in enumerate(blocks):
        owner = lax.rem(s_ref[2] + (ny - offset), ny)
        for z, flip in enumerate(z_order):
            at = pl.multiple_of(((s_ref[3] ^ flip) * ny + owner) * width, width)
            out_ref[:, pl.ds(at, width)] = block[:, z * width : (z + 1) * width]


def place_call(scalars, blocks, z_order):
    rows, tile = blocks[0].shape
    shape = (rows, tile * len(blocks))
    return pl.pallas_call(
        functools.partial(place_kernel, z_order),
        out_shape=jax.ShapeDtypeStruct(shape, blocks[0].dtype),
        grid_spec=pltpu.PrefetchScalarGridSpec(
            num_scalar_prefetch=1,
            grid=(1,),
            in_specs=[whole((rows, tile))] * len(blocks),
            out_specs=whole(shape),
        ),
        compiler_params=pltpu.CompilerParams(vmem_limit_bytes=VMEM_LIMIT),
        cost_estimate=cost(1),
    )(scalars, *blocks)


def on_device(hidden, query, out_grad, attn_out, keys, values, lengths, w_query):
    nz, ny, nx, nc = FACTORS
    plane = ny * nx * nc
    devices = nz * plane
    blk, pb = lax.axis_index("blk"), lax.axis_index("pb")
    core, x_at = lax.rem(pb, nc), lax.rem(pb // nc, nx)
    y_at = lax.rem(pb // (nx * nc), ny)
    offsets = list(dict.fromkeys((1, ny - 1, *range(2, ny - 1))))
    z_at = pb // plane
    place = jnp.stack([core, x_at, y_at, z_at]).astype(jnp.int32)
    y_groups = [
        [z * plane + y * nx * nc + r for y in range(ny)] for z in range(nz) for r in range(nx * nc)
    ]
    z_groups = [[z * plane + r for z in range(nz)] for r in range(plane)]

    def other_blk(x):
        return lax.ppermute(x, "blk", [(0, 1), (1, 0)])

    def other_core(x):
        return lax.ppermute(x, "pb", [(i, i ^ 1) for i in range(devices)])

    def other_x(x):
        return lax.ppermute(x, "pb", [(i, i ^ nc) for i in range(devices)])

    def from_y(x, offset):
        step = nx * nc
        def target(i):
            y = i // step % ny
            return i + ((y - offset) % ny - y) * step
        return lax.ppermute(x, "pb", [(i, target(i)) for i in range(devices)])

    def other_z(x, flip):
        return lax.ppermute(x, "pb", [(i, i ^ (flip * plane)) for i in range(devices)])

    def swap_y(x):
        return lax.all_to_all(
            x, "pb", split_axis=0, concat_axis=0, tiled=True, axis_index_groups=y_groups
        )

    def swap_z(x):
        return lax.all_to_all(
            x, "pb", split_axis=0, concat_axis=0, tiled=True, axis_index_groups=z_groups
        )

    def after(x, *others):
        return lax.optimization_barrier((x, *others))[0]

    tokens = keys.shape[1] * keys.shape[2]
    passages, passage_len = keys.shape[1], keys.shape[2]
    hd = keys.shape[3]
    rows, width = hidden.shape[1], hidden.shape[2]
    part = w_query.shape[0]
    key_rows, value_rows = keys.reshape(tokens, hd), values.reshape(tokens, hd)
    q_own, g_own, o_own = query[0], out_grad[0], attn_out[0]

    q_peer = other_blk(q_own)
    g_peer = other_blk(g_own)

    lens = lengths[0]
    stat_pairs = min(4, hd // PAIR)
    stats_own = stats_call(
        own_stats_kernel, VMEM_WIDE, lens, key_rows, [q_own, g_own, o_own], [], passage_len, stat_pairs
    )
    w_there = other_x(w_query)
    w_near = jnp.where(
        x_at == 0,
        jnp.concatenate([w_query, w_there], axis=0),
        jnp.concatenate([w_there, w_query], axis=0),
    )
    mine = stats_call(
        peer_stats_kernel, VMEM_LIMIT, lens, key_rows, [q_peer], [stats_own], passage_len, stat_pairs
    )
    theirs = other_blk(mine)

    shares = split_call(hidden[0], ny)
    hidden_own = swap_y(after(shares, mine))

    w_mine, flip, z_order = after(w_near, mine)[None], nz // 2, [0]

    def along_z(w_rows, flip, order):
        if flip == 0:
            return w_rows, order
        return jnp.concatenate([w_rows, other_z(w_rows, flip)], axis=0), order + [
            z ^ flip for z in order
        ]

    w_mine, z_order = along_z(w_mine, flip, z_order)

    rows4 = [q_own, q_peer, g_own, g_peer]
    grad_pairs = min(2, hd // PAIR // 2)

    def half_grad(which, carried, dq_type):
        scalars = jnp.concatenate([jnp.reshape(which, (1,)), lens]).astype(jnp.int32)
        return grad_call(scalars, mine, theirs, rows4, key_rows, value_rows, carried, dq_type,
                         passage_len, passages, grad_pairs)

    dq_send, key_part, value_part = half_grad(1 - blk, (), jnp.bfloat16)
    lens = after(lens, w_mine)
    dq_here, key_grad, value_grad = half_grad(blk, (key_part, value_part), jnp.float32)
    dq_there = other_blk(dq_send)
    w_mine, z_order = along_z(w_mine, flip // 2, z_order)
    dq_there, dq_here, hidden_own, w_mine = lax.optimization_barrier(
        (dq_there, dq_here, hidden_own, w_mine)
    )
    qg = (dq_here + dq_there.astype(jnp.float32)).astype(jnp.bfloat16)
    qg = qg.reshape(2 * rows, hd // 2)
    hidden_peer = other_blk(hidden_own)

    arrived = {s: from_y(qg, s) for s in offsets}
    blocks = [qg] + [arrived[s] for s in range(1, ny)]

    w_mine, z_order = along_z(after(w_mine, qg), flip // 4, z_order)

    w_kept, w_given, qg_all = weight_call(
        after(place, w_mine), hidden_own, hidden_peer, blocks, nz, part, max(nz // 4, 1)
    )
    w_other = other_core(w_given)
    w_send = (w_kept[1] + w_other[1].astype(jnp.float32)).astype(jnp.bfloat16)
    w_across = other_x(w_send)
    w_sum = (w_kept[0] + w_other[0].astype(jnp.float32)) + w_across.astype(jnp.float32)

    w_sibling = other_core(after(w_mine, w_send))
    state_kept, state_given = state_call(
        place, w_mine, w_sibling, qg_all, rows, max(nz // 4, 1)
    )
    state_there = other_blk(state_given)
    w_parts = swap_z(w_sum.astype(jnp.bfloat16))
    w_query_grad = jnp.sum(w_parts.astype(jnp.float32), axis=0)
    state_sum = (state_kept + state_there.astype(jnp.float32)).astype(jnp.bfloat16)
    back = [state_sum[0]] + [from_y(state_sum[s], -s) for s in range(1, ny)]
    hidden_grad = place_call(place, back, z_order).reshape(hidden.shape)
    return (hidden_grad, key_grad.reshape(keys.shape), value_grad.reshape(values.shape),
            w_query_grad)


def solution(mesh):
    return jax.shard_map(
        on_device,
        mesh=mesh,
        in_specs=(
            P("pb", "blk", None),
            P("pb", "blk", None),
            P("pb", "blk", None),
            P("pb", "blk", None),
            P("pb", "blk", None, None),
            P("pb", "blk", None, None),
            P("pb", "blk"),
            P("pb", "blk"),
        ),
        out_specs=(
            P("pb", "blk", None),
            P("pb", "blk", None, None),
            P("pb", "blk", None, None),
            P("pb", "blk"),
        ),
        check_vma=False,
    )
```
